256 devices in a mesh: dp: 32 (over x, y, core), tensor: 8 (over z).
Axes of the slice: x: 4, y: 4, z: 8, core: 2. Of those that a mesh axis runs over, the one named last changes fastest.
Arguments:
- activations: bfloat16 [32, 256, 3072], P('dp', None, 'tensor')
- out_grads: bfloat16 [32, 256, 5120], P('dp', 'tensor')
- error_buffer: bfloat16 [32, 3072, 5120], P('dp', 'tensor'), may hold values from -4 to 4
- warm_factor: float32 [5120, 4], replicated, may hold values from -6 to 6
Outputs:
- rebuilt_grad: bfloat16 [3072, 5120], P('tensor')
- next_error: bfloat16 [32, 3072, 5120], P('dp', 'tensor')
- next_factor: float32 [5120, 4], replicated
The draws below stay inside these ranges and needn't reach their ends.
All inputs are finite; a program needn't handle non-finite values.
Results may differ from the reference program's by a relative error of at most 0.00105.
Values may be sent and summed in bfloat16 or wider, within the bound.
A program may use at most 64 MiB of HBM per device.

```python
import math
import jax
import jax.numpy as jnp
from jax import lax

D = 5120
RANK = 4
TOK = 256
ROWS = 3072
N_DP = 32


def draw_activations(key, part):
    key = jax.random.fold_in(key, 11)
    first, second = jax.random.split(key)
    common = jax.random.normal(first, (1, TOK, ROWS), jnp.float32)
    own = jax.random.normal(second, (N_DP, TOK, ROWS), jnp.float32)
    mixed = 0.6 * common + 0.8 * own
    return mixed.astype(jnp.bfloat16)


def draw_out_grads(key, part):
    key = jax.random.fold_in(key, 23)
    first, second, third = jax.random.split(key, 3)
    token_scale = jnp.exp(jax.random.uniform(first, (1, TOK, 1), jnp.float32, 0.0, math.log(10.0)))
    replica_scale = 0.5 + jnp.arange(N_DP, dtype=jnp.float32).reshape(N_DP, 1, 1) / max(N_DP - 1, 1)
    common = jax.random.normal(second, (1, TOK, D), jnp.float32)
    own = jax.random.normal(third, (N_DP, TOK, D), jnp.float32)
    mixed = 0.6 * common + 0.8 * own
    values = 0.25 * token_scale * replica_scale * mixed / math.sqrt(TOK)
    return values.astype(jnp.bfloat16)


def steps_of(rng, shape, cuts, smallest, largest):
    def one(position, parts):
        heights = jax.random.uniform(jax.random.fold_in(jax.random.fold_in(rng, 6), position), (parts,), jnp.float32, smallest / len(cuts), largest / len(cuts))
        return jnp.repeat(jnp.exp(heights), shape[position] // parts).reshape((-1,) + (1,) * (len(shape) - position - 1))

    level = one(*cuts[0])
    for cut in cuts[1:]:
        level = level * one(*cut)
    return level


def noise(stream_key, extent, width, limit, shards=(), kind=jnp.bfloat16):
    factor_of = steps_of(stream_key, extent, shards, -0.22, 0.18) if shards else 1.0
    array = jax.random.normal(stream_key, extent, jnp.float32) * width * factor_of
    return jnp.minimum(jnp.maximum(array, -limit), limit).astype(kind)


def setup_inputs(seed: int = 0) -> dict:
    seeds = jax.random.split(jax.random.key(seed), 5)
    return {
        "activations": draw_activations(jax.random.fold_in(seeds[4], 71), 0),
        "out_grads": draw_out_grads(jax.random.fold_in(seeds[4], 71), 0),
        "error_buffer": noise(seeds[2], (N_DP, ROWS, D), 0.3, 4.0, ((0, 32), (1, 8))),
        "warm_factor": noise(seeds[3], (D, RANK), 1.0, 6.0, (), jnp.float32),
    }


def replica_matrix(activations, out_grads, error_buffer, replica):
    grad = jnp.dot(activations[replica].T.astype(jnp.float32), out_grads[replica].astype(jnp.float32), preferred_element_type=jnp.float32)
    return grad + error_buffer[replica].astype(jnp.float32)

def reference(activations, out_grads, error_buffer, warm_factor):
    high = lax.Precision.HIGHEST

    def left_step(replica, total):
        matrix = replica_matrix(activations, out_grads, error_buffer, replica)
        return total + jnp.dot(matrix, warm_factor, precision=high)
    left_total = lax.fori_loop(0, N_DP, left_step, jnp.zeros((ROWS, RANK), jnp.float32))
    left_mean = left_total / N_DP
    gram = jnp.dot(left_mean.T, left_mean, precision=high)
    lower = jnp.linalg.cholesky(gram)
    left_ortho = lax.linalg.triangular_solve(lower, left_mean, left_side=False, lower=True, transpose_a=True)

    def right_step(replica, total):
        matrix = replica_matrix(activations, out_grads, error_buffer, replica)
        return total + jnp.dot(matrix.T, left_ortho, precision=high)
    right_total = lax.fori_loop(0, N_DP, right_step, jnp.zeros((D, RANK), jnp.float32))
    next_factor = right_total / N_DP
    rebuilt = jnp.dot(left_ortho, next_factor.T, precision=high)

    def new_error(replica):
        matrix = replica_matrix(activations, out_grads, error_buffer, replica)
        return (matrix - rebuilt).astype(jnp.bfloat16)
    next_error = lax.map(new_error, jnp.arange(N_DP, dtype=jnp.int32))
    return (rebuilt.astype(jnp.bfloat16), next_error, next_factor)
```

```python
import functools

import jax
import jax.numpy as jnp
from jax import lax
from jax.experimental import pallas as pl
from jax.experimental.pallas import tpu as pltpu
from jax.sharding import PartitionSpec as P

MESH = pl.DeviceIdType.MESH
F32 = jnp.float32
BF = jnp.bfloat16
DP = 32
NZ = 8
COLS = 640
NN = (((1,), (0,)), ((), ()))
NT = (((1,), (1,)), ((), ()))
TN = (((0,), (0,)), ((), ()))

RIGHT_HOPS = {0: 3, 1: 4, 2: 4, 3: 4, 4: 4, 5: 3, 6: 3, 7: 3}
RIGHT_FIRST = (4, 3, 2, 1)
RIGHT_REST = (0, 7, 6, 5)
LEFT_FIRST = (5, 6, 7)
LEFT_REST = (0, 1, 2, 3, 4)


def hops(direction, k):
    return RIGHT_HOPS[k] if direction == 0 else 7 - RIGHT_HOPS[k]


def dot(a, b, dims):
    return lax.dot_general(a, b, dims, preferred_element_type=F32)


def split16(x):
    r = jnp.concatenate([x, x, x, x], axis=0)
    high = r.astype(BF).astype(F32)
    rest = r - high
    middle = rest.astype(BF).astype(F32)
    low = rest - middle
    row = lax.broadcasted_iota(jnp.int32, r.shape, 0)
    out = jnp.where(row < 4, high, jnp.where(row < 8, middle, jnp.where(row < 12, low, 0.0)))
    return out.astype(BF)


def fold(x):
    return x[0:4] + x[4:8] + x[8:12]


def parts3(x):
    high = x.astype(BF).astype(F32)
    rest = x - high
    middle = rest.astype(BF).astype(F32)
    return high, middle, rest - middle


def chain_kernel(a_hbm, g_hbm, e_hbm, w_hbm, m_ref, nx_ref, lx_ref,
                 a_ref, e_ref, w_ref, g_all, we_ref,
                 p_send, p_buf, l_send, l_buf, z_send, z_buf, r_send, r_buf, n_send, n_buf,
                 load_sem, g_ssem, g_rsem, z_ssem, z_rsem, d_ssem, d_rsem):
    t = lax.axis_index("tensor")
    r = lax.axis_index("dp")
    right, left = lax.rem(t + 1, NZ), lax.rem(t + NZ - 1, NZ)

    barrier = pltpu.get_barrier_semaphore()
    for k in (4, 5, 3, 6, 2, 7, 1):
        pl.semaphore_signal(barrier, inc=1, device_id={"tensor": lax.rem(t + k, NZ)}, device_id_type=MESH)

    def greet(k, carry):
        pl.semaphore_signal(barrier, inc=1, device_id={"dp": lax.rem(r + k, DP)}, device_id_type=MESH)
        return carry

    load_g = pltpu.make_async_copy(g_hbm, g_all.at[pl.ds(pl.multiple_of(t * 32, 32), 32)], load_sem.at[0])
    load_w = pltpu.make_async_copy(w_hbm, w_ref, load_sem.at[1])
    load_a = pltpu.make_async_copy(a_hbm, a_ref, load_sem.at[2])
    load_e = pltpu.make_async_copy(e_hbm, e_ref, load_sem.at[3])
    for c in (load_g, load_w, load_e, load_a):
        c.start()
    lax.fori_loop(1, DP, greet, 0, unroll=True)

    def g_copy(d, s, k):
        origin = lax.rem(t + NZ - s, NZ) if d == 0 else lax.rem(t + s, NZ)
        return _g_copy(origin, d, s, k)

    def _g_copy(origin, d, s, k):
        col = pl.multiple_of(lax.rem(origin + k, NZ) * COLS, COLS)
        ref = g_all.at[pl.ds(pl.multiple_of(origin * 32, 32), 32), pl.ds(col, COLS)]
        return pltpu.make_async_remote_copy(
            ref, ref, g_ssem.at[d, s, k], g_rsem.at[d, s, k],
            device_id={"tensor": (right, left)[d]}, device_id_type=MESH)

    def g_recv(d, s, k):
        if s >= hops(d, k):
            return
        origin = lax.rem(t + NZ - s - 1, NZ) if d == 0 else lax.rem(t + s + 1, NZ)
        _g_copy(origin, d, s, k).wait_recv()
        if s + 1 < hops(d, k):
            _g_copy(origin, d, s + 1, k).start()

    def z_exchange(i, send_of, buf):
        for k in (4, 5, 3, 6, 2, 7, 1):
            to = lax.rem(t + k, NZ)
            pltpu.make_async_remote_copy(send_of(to), buf.at[t], z_ssem.at[i], z_rsem.at[i],
                                         device_id={"tensor": to}, device_id_type=MESH).start()

    def z_wait(i, buf):
        w = buf.at[pl.ds(0, NZ - 1)]
        pltpu.make_async_copy(w, w, z_rsem.at[i]).wait()

    def dp_exchange(i, send, buf):
        def one(k, carry):
            pltpu.make_async_remote_copy(send, buf.at[r], d_ssem.at[i], d_rsem.at[i],
                                         device_id={"dp": lax.rem(r + k, DP)}, device_id_type=MESH).start()
            return carry
        lax.fori_loop(1, DP, one, 0, unroll=True)

    def dp_wait(i, buf):
        w = buf.at[pl.ds(0, DP - 1)]
        pltpu.make_async_copy(w, w, d_rsem.at[i]).wait()

    load_w.wait()
    we_ref[...] = split16(w_ref[...])
    load_g.wait()
    g_own = g_all[pl.ds(pl.multiple_of(t * 32, 32), 32), :]
    p = fold(dot(we_ref[...], g_own, NT))
    wide = jnp.concatenate([p] * NZ, axis=1)
    lane = lax.broadcasted_iota(jnp.int32, (4, 256), 1)
    wide = jnp.where(lane // 32 == t, wide, 0.0)
    p_send[...] = wide
    p_buf[t] = wide

    pl.semaphore_wait(barrier, DP - 1 + NZ - 1)

    z_exchange(0, lambda to: p_send, p_buf)
    for k in RIGHT_FIRST:
        g_copy(0, 0, k).start()
    for k in LEFT_FIRST:
        g_copy(1, 0, k).start()

    load_e.wait()
    left_e = jnp.zeros((16, 384), F32)
    for c in range(NZ):
        cols = pl.ds(c * COLS, COLS)
        left_e = left_e + dot(we_ref[:, cols], e_ref[:, cols], NT)
    load_a.wait()

    for k in RIGHT_FIRST:
        g_recv(0, 0, k)
    for k in LEFT_FIRST:
        g_recv(1, 0, k)
    for k in RIGHT_REST:
        g_copy(0, 0, k).start()
    for k in LEFT_REST:
        g_copy(1, 0, k).start()

    z_wait(0, p_buf)
    p_all = p_buf[0]
    for i in range(1, NZ):
        p_all = p_all + p_buf[i]
    left_part = fold(left_e) + fold(dot(split16(p_all), a_ref[...], NN))
    l_send[...] = left_part
    l_buf[r] = left_part
    dp_exchange(0, l_send, l_buf)

    for s in (1, 2):
        for k in RIGHT_FIRST:
            if k > s:
                g_recv(0, s, k)
        for k in LEFT_FIRST:
            if 8 - k > s:
                g_recv(1, s, k)

    dp_wait(0, l_buf)
    lm = l_buf[0]
    for i in range(1, DP):
        lm = lm + l_buf[i]
    lm = lm * (1.0 / DP)
    peak = jnp.maximum(jnp.max(jnp.max(jnp.abs(lm), axis=1, keepdims=True), axis=0, keepdims=True), 1e-30)
    lm = lm / peak
    l16 = split16(lm)
    gram = fold(dot(l16, l16, NT))
    gram = gram[:, 0:4] + gram[:, 4:8] + gram[:, 8:12]
    info = jnp.concatenate([gram, jnp.broadcast_to(peak, (4, 124))], axis=1)
    q = fold(dot(l16, a_ref[...], NT))
    for c in range(NZ):
        z_send[c, :, 640:896] = q
        z_send[c, :, 896:1024] = info
        z_send[c, :, 0:640] = fold(dot(l16, e_ref[:, c * COLS:(c + 1) * COLS], NN))
    z_exchange(1, lambda to: z_send.at[to], z_buf)
    z_buf[t] = z_send[t]

    for k in (4,):
        g_recv(0, 3, k)

    z_wait(1, z_buf)
    peaks = [z_buf[i, :, 1000:1001] for i in range(NZ)]
    top = peaks[0]
    for i in range(1, NZ):
        top = jnp.maximum(top, peaks[i])
    scales = [x / top for x in peaks]
    total = z_buf[0, :, 0:896] * scales[0]
    gram = z_buf[0, :, 896:900] * (scales[0] * scales[0])
    for i in range(1, NZ):
        total = total + z_buf[i, :, 0:896] * scales[i]
        gram = gram + z_buf[i, :, 896:900] * (scales[i] * scales[i])
    mine = pl.ds(pl.multiple_of(t * COLS, COLS), COLS)
    right_part = total[:, 0:640] + fold(dot(split16(total[:, 640:896]), g_all[:, mine], NN))
    r_send[...] = right_part
    r_buf[r] = right_part
    dp_exchange(1, r_send, r_buf)

    lower = [[None] * 4 for _ in range(4)]
    for i in range(4):
        for j in range(i + 1):
            v = gram[i:i + 1, j:j + 1]
            for k in range(j):
                v = v - lower[i][k] * lower[j][k]
            lower[i][j] = jnp.sqrt(v) if i == j else v / lower[j][j]

    def solve(rows):
        out = []
        for j in range(4):
            v = rows[j]
            for i in range(j):
                v = v - out[i] * lower[j][i]
            out.append(v / lower[j][j])
        return jnp.concatenate(out, axis=0)

    own_scale = peak / top[0:1]
    lm = lm * own_scale
    lo = solve([lm[j:j + 1] for j in range(4)])
    high, middle, low = parts3(lo)
    zero = jnp.zeros_like(lo)
    lx_ref[...] = jnp.concatenate([high, high, middle, middle, high, low, zero, zero], axis=0).astype(BF)

    rest = [(d, s, k) for s in range(4) for d, k in
            [(0, k) for k in RIGHT_FIRST + RIGHT_REST] + [(1, k) for k in LEFT_FIRST + LEFT_REST]]
    done = {(0, 0, k) for k in RIGHT_FIRST} | {(1, 0, k) for k in LEFT_FIRST}
    done |= {(0, s, k) for s in (1, 2) for k in RIGHT_FIRST if k > s}
    done |= {(1, s, k) for s in (1, 2) for k in LEFT_FIRST if 8 - k > s}
    done |= {(0, 3, 4)}
    rest = [x for x in rest if x not in done]
    for x in rest[:14]:
        g_recv(*x)

    dp_wait(1, r_buf)
    nr = r_buf[0]
    for i in range(1, DP):
        nr = nr + r_buf[i]
    nr = nr * (1.0 / DP)
    n_send[...] = nr
    n_buf[t] = nr
    z_exchange(2, lambda to: n_send, n_buf)

    for x in rest[14:]:
        g_recv(*x)

    at = jnp.transpose(a_ref[...])
    for c in range(NZ):
        cols = slice(c * COLS, (c + 1) * COLS)
        m_ref[:, cols] = dot(at, g_all[:, cols], NN) + e_ref[:, cols].astype(F32)

    z_wait(2, n_buf)
    for c in range(NZ):
        x = n_buf[c]
        nx_ref[:, c * COLS:(c + 1) * COLS] = solve([x[j:j + 1] for j in range(4)])

    for d in range(2):
        for k in range(NZ):
            for s in range(hops(d, k)):
                g_copy(d, s, k).wait_send()
    for i, buf in enumerate((p_buf, z_buf, n_buf)):
        w = buf.at[pl.ds(0, NZ - 1)]
        pltpu.make_async_copy(w, w, z_ssem.at[i]).wait()
    for i, buf in enumerate((l_buf, r_buf)):
        w = buf.at[pl.ds(0, DP - 1)]
        pltpu.make_async_copy(w, w, d_ssem.at[i]).wait()


def finish_kernel(m_ref, n_ref, lx_ref, rebuilt_hbm, error_hbm, nout_ref, out_a, out_b, sem):
    lxt = lx_ref[...]
    nout_ref[...] = n_ref[...]
    copies = []
    for c in range(NZ):
        cols = slice(c * COLS, (c + 1) * COLS)
        high, middle, low = parts3(n_ref[:, cols])
        zero = jnp.zeros_like(high)
        nx = jnp.concatenate([high, middle, high, middle, low, high, zero, zero], axis=0).astype(BF)
        rebuilt = dot(lxt, nx, TN)
        out_a[:, cols] = rebuilt.astype(BF)
        out_b[:, cols] = (m_ref[:, cols] - rebuilt).astype(BF)
        for i, (src, dst) in enumerate(((out_a, rebuilt_hbm), (out_b, error_hbm))):
            cp = pltpu.make_async_copy(src.at[:, cols], dst.at[:, cols], sem.at[i, c])
            cp.start()
            copies.append(cp)
    for cp in copies:
        cp.wait()


def per_device(activations, out_grads, error_buffer, warm_factor):
    any_spec = pl.BlockSpec(memory_space=pl.ANY)
    vmem = pl.BlockSpec(memory_space=pltpu.VMEM)
    V = pltpu.VMEM
    D = pltpu.SemaphoreType.DMA
    m, n, lx = pl.pallas_call(
        chain_kernel,
        out_shape=OUT_SHAPES(),
        in_specs=[any_spec] * 4,
        out_specs=[vmem] * 3,
        scratch_shapes=[
            V((256, 384), BF), V((384, 5120), BF), V((4, 5120), F32), V((256, 5120), BF), V((16, 5120), BF),
            V((4, 256), F32), V((NZ, 4, 256), F32), V((4, 384), F32), V((DP, 4, 384), F32),
            V((NZ, 4, 1024), F32), V((NZ, 4, 1024), F32), V((4, 640), F32), V((DP, 4, 640), F32),
            V((4, 640), F32), V((NZ, 4, 640), F32),
            D((4,)), D((2, 4, NZ)), D((2, 4, NZ)), D((3,)), D((3,)), D((2,)), D((2,)),
        ],
        compiler_params=pltpu.CompilerParams(collective_id=0, has_side_effects=True, vmem_limit_bytes=32 << 20),
    )(activations[0], out_grads[0], error_buffer[0], warm_factor.T)
    rebuilt, error, factor = pl.pallas_call(
        finish_kernel,
        out_shape=[jax.ShapeDtypeStruct((384, 5120), BF), jax.ShapeDtypeStruct((384, 5120), BF),
                   jax.ShapeDtypeStruct((4, 5120), F32)],
        in_specs=[vmem] * 3,
        out_specs=[any_spec, any_spec, vmem],
        scratch_shapes=[V((384, 5120), BF), V((384, 5120), BF), D((2, NZ))],
        compiler_params=pltpu.CompilerParams(vmem_limit_bytes=32 << 20),
    )(m, n, lx)
    return rebuilt, error[None], factor.T


def OUT_SHAPES():
    return [jax.ShapeDtypeStruct((384, 5120), F32), jax.ShapeDtypeStruct((4, 5120), F32),
            jax.ShapeDtypeStruct((32, 384), BF)]


def solution(mesh):
    return jax.shard_map(
        per_device,
        mesh=mesh,
        in_specs=(P("dp", None, "tensor"), P("dp", "tensor", None), P("dp", "tensor", None), P()),
        out_specs=(P("tensor", None), P("dp", "tensor", None), P()),
        check_vma=False,
    )
```

```python
import functools

import jax
import jax.numpy as jnp
from jax import lax
from jax.experimental import pallas as pl
from jax.experimental.pallas import tpu as pltpu
from jax.sharding import PartitionSpec as P

MESH = pl.DeviceIdType.MESH
F32 = jnp.float32
BF = jnp.bfloat16
DP = 32
NZ = 8
COLS = 640
NN = (((1,), (0,)), ((), ()))
NT = (((1,), (1,)), ((), ()))
TN = (((0,), (0,)), ((), ()))

RIGHT_HOPS = {0: 3, 1: 4, 2: 4, 3: 4, 4: 4, 5: 3, 6: 3, 7: 3}
CHIPS = 16
FAR_FIRST = sorted(((dx, dy) for dx in range(4) for dy in range(4) if dx or dy),
                   key=lambda v: -(min(v[0], 4 - v[0]) + min(v[1], 4 - v[1])))
GATHER = {
    "start": ((0, -1, (4, 3, 2, 1)), (1, -1, (5, 6, 7)), (0, -1, (0, 7)), (1, -1, (0, 4, 3))),
    "left": ((0, 0, (4, 3)), (1, 0, (5,))),
    "pair0": ((0, 0, (2,)), (1, 0, (6,)), (0, -1, (6, 5)), (1, -1, (2, 1))),
    "sent0": ((0, 1, (4, 3)), (1, 1, (5,)), (0, 0, (1, 0)), (1, 0, (7, 0))),
    "sums": ((0, 2, (4,)), (0, 0, (7, 6, 5)), (1, 0, (4, 3, 2, 1)), (0, 1, (2, 1)), (1, 1, (6, 7))),
    "mine": ((0, 3, (4,)), (0, 2, (3,)), (1, 2, (5,)), (0, 1, (0,)), (1, 1, (0,))),
    "pair1": ((0, 1, (7,)), (1, 1, (4,))),
    "sent1": ((0, 1, (6, 5)), (1, 1, (3, 2, 1)), (0, 2, (2, 1)), (1, 2, (6, 7, 0))),
    "rest": ((0, 2, (0, 7, 6, 5)), (1, 2, (4, 3, 2, 1)), (0, 3, (3, 2, 1)), (1, 3, (5, 6, 7, 0))),
}

def hops(direction, k):
    return RIGHT_HOPS[k] if direction == 0 else 7 - RIGHT_HOPS[k]


def dot(a, b, dims):
    return lax.dot_general(a, b, dims, preferred_element_type=F32)


def split16(x):
    r = jnp.concatenate([x, x, x, x], axis=0)
    high = r.astype(BF).astype(F32)
    rest = r - high
    middle = rest.astype(BF).astype(F32)
    low = rest - middle
    row = lax.broadcasted_iota(jnp.int32, r.shape, 0)
    out = jnp.where(row < 4, high, jnp.where(row < 8, middle, jnp.where(row < 12, low, 0.0)))
    return out.astype(BF)


def fold(x):
    return x[0:4] + x[4:8] + x[8:12]


def parts3(x):
    high = x.astype(BF).astype(F32)
    rest = x - high
    middle = rest.astype(BF).astype(F32)
    return high, middle, rest - middle


def chain_kernel(a_hbm, g_hbm, e_hbm, w_hbm, m_ref, nx_ref, lx_ref,
                 a_ref, e_ref, w_ref, g_all, we_ref,
                 p_send, p_buf, l_pair, l_send, l_buf, z_send, z_buf, r_pair, r_send, r_buf, n_send, n_buf,
                 load_sem, g_ssem, g_rsem, z_ssem, z_rsem, d_ssem, d_rsem, pair_ssem, pair_rsem):
    t = lax.axis_index("tensor")
    r = lax.axis_index("dp")
    right, left = lax.rem(t + 1, NZ), lax.rem(t + NZ - 1, NZ)
    x, y, core = r // 8, lax.rem(r // 2, 4), lax.rem(r, 2)
    chip = r // 2
    sibling = r + 1 - 2 * core

    barrier = pltpu.get_barrier_semaphore()
    for k in (4, 5, 3, 6, 2, 7, 1):
        pl.semaphore_signal(barrier, inc=1, device_id={"tensor": lax.rem(t + k, NZ)}, device_id_type=MESH)

    load_g = pltpu.make_async_copy(g_hbm, g_all.at[pl.ds(pl.multiple_of(t * 32, 32), 32)], load_sem.at[0])
    load_w = pltpu.make_async_copy(w_hbm, w_ref, load_sem.at[1])
    load_a = pltpu.make_async_copy(a_hbm, a_ref, load_sem.at[2])
    load_e = pltpu.make_async_copy(e_hbm, e_ref, load_sem.at[3])
    for c in (load_g, load_w, load_e, load_a):
        c.start()
    for dx, dy in FAR_FIRST:
        to = lax.rem(x + dx, 4) * 8 + lax.rem(y + dy, 4) * 2 + core
        pl.semaphore_signal(barrier, inc=1, device_id={"dp": to}, device_id_type=MESH)
    pl.semaphore_signal(barrier, inc=1, device_id={"dp": sibling}, device_id_type=MESH)

    def g_copy(d, s, k):
        origin = lax.rem(t + NZ - s, NZ) if d == 0 else lax.rem(t + s, NZ)
        return _g_copy(origin, d, s, k)

    def _g_copy(origin, d, s, k):
        col = pl.multiple_of(lax.rem(origin + k, NZ) * COLS, COLS)
        ref = g_all.at[pl.ds(pl.multiple_of(origin * 32, 32), 32), pl.ds(col, COLS)]
        return pltpu.make_async_remote_copy(
            ref, ref, g_ssem.at[d, s, k], g_rsem.at[d, s, k],
            device_id={"tensor": (right, left)[d]}, device_id_type=MESH)

    def g_recv(d, s, k):
        if s >= hops(d, k):
            return
        origin = lax.rem(t + NZ - s - 1, NZ) if d == 0 else lax.rem(t + s + 1, NZ)
        _g_copy(origin, d, s, k).wait_recv()
        if s + 1 < hops(d, k):
            _g_copy(origin, d, s + 1, k).start()

    def gather(point):
        for d, s, chunks in GATHER[point]:
            for k in chunks:
                if s < 0:
                    g_copy(d, 0, k).start()
                else:
                    g_recv(d, s, k)

    def z_exchange(i, send_of, buf):
        for k in (4, 5, 3, 6, 2, 7, 1):
            to = lax.rem(t + k, NZ)
            pltpu.make_async_remote_copy(send_of(to), buf.at[t], z_ssem.at[i], z_rsem.at[i],
                                         device_id={"tensor": to}, device_id_type=MESH).start()

    def z_wait(i, buf):
        w = buf.at[pl.ds(0, NZ - 1)]
        pltpu.make_async_copy(w, w, z_rsem.at[i]).wait()

    def pair_copy(i, send, buf):
        return pltpu.make_async_remote_copy(send, buf, pair_ssem.at[i], pair_rsem.at[i],
                                            device_id={"dp": sibling}, device_id_type=MESH)

    def dp_exchange(i, send, buf):
        for dx, dy in FAR_FIRST:
            to = lax.rem(x + dx, 4) * 8 + lax.rem(y + dy, 4) * 2 + core
            pltpu.make_async_remote_copy(send, buf.at[chip], d_ssem.at[i], d_rsem.at[i],
                                         device_id={"dp": to}, device_id_type=MESH).start()

    def dp_wait(i, buf):
        w = buf.at[pl.ds(0, CHIPS - 1)]
        pltpu.make_async_copy(w, w, d_rsem.at[i]).wait()

    load_w.wait()
    we_ref[...] = split16(w_ref[...])
    load_g.wait()
    g_own = g_all[pl.ds(pl.multiple_of(t * 32, 32), 32), :]
    p = fold(dot(we_ref[...], g_own, NT))
    wide = jnp.concatenate([p] * NZ, axis=1)
    lane = lax.broadcasted_iota(jnp.int32, (4, 256), 1)
    wide = jnp.where(lane // 32 == t, wide, 0.0)
    p_send[...] = wide
    p_buf[t] = wide

    pl.semaphore_wait(barrier, CHIPS + NZ - 1)

    z_exchange(0, lambda to: p_send, p_buf)
    gather("start")

    load_e.wait()
    left_e = jnp.zeros((16, 384), F32)
    for c in range(NZ):
        cols = pl.ds(c * COLS, COLS)
        left_e = left_e + dot(we_ref[:, cols], e_ref[:, cols], NT)
    load_a.wait()

    gather("left")

    z_wait(0, p_buf)
    p_all = p_buf[0]
    for i in range(1, NZ):
        p_all = p_all + p_buf[i]
    left_part = fold(left_e) + fold(dot(split16(p_all), a_ref[...], NN))
    l_pair[0] = left_part
    pair_copy(0, l_pair.at[0], l_pair.at[1]).start()
    gather("pair0")
    pair_copy(0, l_pair.at[0], l_pair.at[1]).wait_recv()
    left_part = left_part + l_pair[1]
    l_send[...] = left_part
    l_buf[chip] = left_part
    dp_exchange(0, l_send, l_buf)
    gather("sent0")

    dp_wait(0, l_buf)
    lm = l_buf[0]
    for i in range(1, CHIPS):
        lm = lm + l_buf[i]
    lm = lm * (1.0 / DP)
    peak = jnp.maximum(jnp.max(jnp.max(jnp.abs(lm), axis=1, keepdims=True), axis=0, keepdims=True), 1e-30)
    lm = lm / peak
    l16 = split16(lm)
    gram = fold(dot(l16, l16, NT))
    gram = gram[:, 0:4] + gram[:, 4:8] + gram[:, 8:12]
    info = jnp.concatenate([gram, jnp.broadcast_to(peak, (4, 124))], axis=1)
    q = fold(dot(l16, a_ref[...], NT))
    for c in range(NZ):
        z_send[c, :, 640:896] = q
        z_send[c, :, 896:1024] = info
        z_send[c, :, 0:640] = fold(dot(l16, e_ref[:, c * COLS:(c + 1) * COLS], NN))
    z_exchange(1, lambda to: z_send.at[to], z_buf)
    z_buf[t] = z_send[t]

    gather("sums")

    z_wait(1, z_buf)
    peaks = [z_buf[i, :, 1000:1001] for i in range(NZ)]
    top = peaks[0]
    for i in range(1, NZ):
        top = jnp.maximum(top, peaks[i])
    scales = [x / top for x in peaks]
    total = z_buf[0, :, 0:896] * scales[0]
    gram = z_buf[0, :, 896:900] * (scales[0] * scales[0])
    for i in range(1, NZ):
        total = total + z_buf[i, :, 0:896] * scales[i]
        gram = gram + z_buf[i, :, 896:900] * (scales[i] * scales[i])
    gather("mine")
    mine = pl.ds(pl.multiple_of(t * COLS, COLS), COLS)
    right_part = total[:, 0:640] + fold(dot(split16(total[:, 640:896]), g_all[:, mine], NN))
    r_pair[0] = right_part
    pair_copy(1, r_pair.at[0], r_pair.at[1]).start()
    gather("pair1")
    pair_copy(1, r_pair.at[0], r_pair.at[1]).wait_recv()
    right_part = right_part + r_pair[1]
    r_send[...] = right_part
    r_buf[chip] = right_part
    dp_exchange(1, r_send, r_buf)

    lower = [[None] * 4 for _ in range(4)]
    for i in range(4):
        for j in range(i + 1):
            v = gram[i:i + 1, j:j + 1]
            for k in range(j):
                v = v - lower[i][k] * lower[j][k]
            lower[i][j] = jnp.sqrt(v) if i == j else v / lower[j][j]

    def solve(rows):
        out = []
        for j in range(4):
            v = rows[j]
            for i in range(j):
                v = v - out[i] * lower[j][i]
            out.append(v / lower[j][j])
        return jnp.concatenate(out, axis=0)

    own_scale = peak / top[0:1]
    lm = lm * own_scale
    lo = solve([lm[j:j + 1] for j in range(4)])
    high, middle, low = parts3(lo)
    zero = jnp.zeros_like(lo)
    lx_ref[...] = jnp.concatenate([high, high, middle, middle, high, low, zero, zero], axis=0).astype(BF)

    gather("sent1")
    dp_wait(1, r_buf)
    nr = r_buf[0]
    for i in range(1, CHIPS):
        nr = nr + r_buf[i]
    nr = nr * (1.0 / DP)
    n_send[...] = nr
    n_buf[t] = nr
    z_exchange(2, lambda to: n_send, n_buf)

    gather("rest")

    at = jnp.transpose(a_ref[...])
    for c in range(NZ):
        cols = slice(c * COLS, (c + 1) * COLS)
        m_ref[:, cols] = dot(at, g_all[:, cols], NN) + e_ref[:, cols].astype(F32)

    z_wait(2, n_buf)
    for c in range(NZ):
        x = n_buf[c]
        nx_ref[:, c * COLS:(c + 1) * COLS] = solve([x[j:j + 1] for j in range(4)])

    for d in range(2):
        for k in range(NZ):
            for s in range(hops(d, k)):
                g_copy(d, s, k).wait_send()
    for i, buf in enumerate((p_buf, z_buf, n_buf)):
        w = buf.at[pl.ds(0, NZ - 1)]
        pltpu.make_async_copy(w, w, z_ssem.at[i]).wait()
    pair_copy(0, l_pair.at[0], l_pair.at[1]).wait_send()
    pair_copy(1, r_pair.at[0], r_pair.at[1]).wait_send()
    for i, buf in enumerate((l_buf, r_buf)):
        w = buf.at[pl.ds(0, CHIPS - 1)]
        pltpu.make_async_copy(w, w, d_ssem.at[i]).wait()


def finish_kernel(m_ref, n_ref, lx_ref, rebuilt_hbm, error_hbm, nout_ref, out_a, out_b, sem):
    lxt = lx_ref[...]
    nout_ref[...] = n_ref[...]
    copies = []
    for c in range(NZ):
        cols = slice(c * COLS, (c + 1) * COLS)
        high, middle, low = parts3(n_ref[:, cols])
        zero = jnp.zeros_like(high)
        nx = jnp.concatenate([high, middle, high, middle, low, high, zero, zero], axis=0).astype(BF)
        rebuilt = dot(lxt, nx, TN)
        out_a[:, cols] = rebuilt.astype(BF)
        out_b[:, cols] = (m_ref[:, cols] - rebuilt).astype(BF)
        for i, (src, dst) in enumerate(((out_a, rebuilt_hbm), (out_b, error_hbm))):
            cp = pltpu.make_async_copy(src.at[:, cols], dst.at[:, cols], sem.at[i, c])
            cp.start()
            copies.append(cp)
    for cp in copies:
        cp.wait()


def per_device(activations, out_grads, error_buffer, warm_factor):
    any_spec = pl.BlockSpec(memory_space=pl.ANY)
    hbm_spec = pl.BlockSpec(memory_space=pltpu.HBM)
    vmem = pl.BlockSpec(memory_space=pltpu.VMEM)
    V = pltpu.VMEM
    D = pltpu.SemaphoreType.DMA
    m, n, lx = pl.pallas_call(
        chain_kernel,
        out_shape=OUT_SHAPES(),
        in_specs=[hbm_spec] * 4,
        out_specs=[vmem] * 3,
        scratch_shapes=[
            V((256, 384), BF), V((384, 5120), BF), V((4, 5120), F32), V((256, 5120), BF), V((16, 5120), BF),
            V((4, 256), F32), V((NZ, 4, 256), F32), V((2, 4, 384), F32), V((4, 384), F32), V((CHIPS, 4, 384), F32),
            V((NZ, 4, 1024), F32), V((NZ, 4, 1024), F32), V((2, 4, 640), F32), V((4, 640), F32), V((CHIPS, 4, 640), F32),
            V((4, 640), F32), V((NZ, 4, 640), F32),
            D((4,)), D((2, 4, NZ)), D((2, 4, NZ)), D((3,)), D((3,)), D((2,)), D((2,)), D((2,)), D((2,)),
        ],
        compiler_params=pltpu.CompilerParams(collective_id=0, has_side_effects=True, vmem_limit_bytes=32 << 20),
    )(*(pltpu.with_memory_space_constraint(x, pltpu.HBM)
        for x in (activations[0], out_grads[0], error_buffer[0], warm_factor.T)))
    rebuilt, error, factor = pl.pallas_call(
        finish_kernel,
        out_shape=[jax.ShapeDtypeStruct((384, 5120), BF), jax.ShapeDtypeStruct((384, 5120), BF),
                   jax.ShapeDtypeStruct((4, 5120), F32)],
        in_specs=[vmem] * 3,
        out_specs=[any_spec, any_spec, vmem],
        scratch_shapes=[V((384, 5120), BF), V((384, 5120), BF), D((2, NZ))],
        compiler_params=pltpu.CompilerParams(vmem_limit_bytes=32 << 20),
    )(m, n, lx)
    return rebuilt, error[None], factor.T


def OUT_SHAPES():
    return [jax.ShapeDtypeStruct((384, 5120), F32), jax.ShapeDtypeStruct((4, 5120), F32),
            jax.ShapeDtypeStruct((32, 384), BF)]


def solution(mesh):
    return jax.shard_map(
        per_device,
        mesh=mesh,
        in_specs=(P("dp", None, "tensor"), P("dp", "tensor", None), P("dp", "tensor", None), P()),
        out_specs=(P("tensor", None), P("dp", "tensor", None), P()),
        check_vma=False,
    )
```

```python
import functools

import jax
import jax.numpy as jnp
from jax import lax
from jax.experimental import pallas as pl
from jax.experimental.pallas import tpu as pltpu
from jax.sharding import PartitionSpec as P

MESH = pl.DeviceIdType.MESH
F32 = jnp.float32
BF = jnp.bfloat16
DP = 32
NZ = 8
COLS = 640
NN = (((1,), (0,)), ((), ()))
NT = (((1,), (1,)), ((), ()))
TN = (((0,), (0,)), ((), ()))

RIGHT_HOPS = {0: 3, 1: 4, 2: 4, 3: 4, 4: 4, 5: 3, 6: 3, 7: 3}
CHIPS = 16
FAR_FIRST = sorted(((dx, dy) for dx in range(4) for dy in range(4) if dx or dy),
                   key=lambda v: -(min(v[0], 4 - v[0]) + min(v[1], 4 - v[1])))
GATHER = {
    "start": ((0, -1, (4, 3, 2, 1, )), (1, -1, (5, 6, 7, )), (0, -1, (0, 7, )), (1, -1, (0, 4, 3, ))),
    "middle": (),
    "left": ((0, 0, (4, 3, )), (1, 0, (5, ))),
    "pair0": ((0, 0, (2, )), (1, 0, (6, )), (0, -1, (6, 5, )), (1, -1, (2, 1, ))),
    "sent0": ((0, 1, (4, 3, )), (1, 1, (5, )), (0, 0, (1, 0, )), (1, 0, (7, 0, ))),
    "prepare2": (),
    "prepare4": (),
    "sums": ((0, 2, (4, )), (0, 0, (7, 6, 5, )), (1, 0, (4, 3, 2, 1, )), (0, 1, (2, 1, )), (1, 1, (6, 7, ))),
    "mine": ((0, 3, (4, )), (0, 2, (3, )), (1, 2, (5, )), (0, 1, (0, )), (1, 1, (0, ))),
    "pair1": ((0, 1, (7, )), (1, 1, (4, ))),
    "sent1": ((0, 1, (6, 5, )), (1, 1, (3, 2, 1, )), (0, 2, (2, 1, )), (1, 2, (6, 7, 0, ))),
    "rest": ((0, 2, (0, 7, 6, 5, )), (1, 2, (4, 3, 2, 1, ))),
}


def hops(direction, k):
    return RIGHT_HOPS[k] if direction == 0 else 7 - RIGHT_HOPS[k]


def dot(a, b, dims):
    return lax.dot_general(a, b, dims, preferred_element_type=F32)


def split16(x):
    r = jnp.concatenate([x, x, x, x], axis=0)
    high = r.astype(BF).astype(F32)
    rest = r - high
    middle = rest.astype(BF).astype(F32)
    low = rest - middle
    row = lax.broadcasted_iota(jnp.int32, r.shape, 0)
    out = jnp.where(row < 4, high, jnp.where(row < 8, middle, jnp.where(row < 12, low, 0.0)))
    return out.astype(BF)


def fold(x):
    return x[0:4] + x[4:8] + x[8:12]


def parts3(x):
    high = x.astype(BF).astype(F32)
    rest = x - high
    middle = rest.astype(BF).astype(F32)
    return high, middle, rest - middle


def chain_kernel(a_hbm, g_hbm, e_hbm, w_hbm, m_ref, nx_ref, lx_ref, ch_ref,
                 a_ref, at_ref, e_ref, w_ref, g_all, we_ref,
                 p_send, p_buf, l_pair, l_send, l_buf, z_send, z_buf, r_pair, r_send, r_buf, n_send, n_buf,
                 load_sem, g_ssem, g_rsem, z_ssem, z_rsem, d_ssem, d_rsem, pair_ssem, pair_rsem):
    t = lax.axis_index("tensor")
    r = lax.axis_index("dp")
    right, left = lax.rem(t + 1, NZ), lax.rem(t + NZ - 1, NZ)
    x, y, core = r // 8, lax.rem(r // 2, 4), lax.rem(r, 2)
    chip = r // 2
    sibling = r + 1 - 2 * core

    barrier = pltpu.get_barrier_semaphore()
    for k in (4, 5, 3, 6, 2, 7, 1):
        pl.semaphore_signal(barrier, inc=1, device_id={"tensor": lax.rem(t + k, NZ)}, device_id_type=MESH)

    load_g = pltpu.make_async_copy(g_hbm, g_all.at[pl.ds(pl.multiple_of(t * 32, 32), 32)], load_sem.at[0])
    load_w = pltpu.make_async_copy(w_hbm, w_ref, load_sem.at[1])
    load_a = pltpu.make_async_copy(a_hbm, a_ref, load_sem.at[2])
    load_e = pltpu.make_async_copy(e_hbm, e_ref, load_sem.at[3])
    for c in (load_g, load_w, load_e, load_a):
        c.start()
    for dx, dy in FAR_FIRST:
        to = lax.rem(x + dx, 4) * 8 + lax.rem(y + dy, 4) * 2 + core
        pl.semaphore_signal(barrier, inc=1, device_id={"dp": to}, device_id_type=MESH)
    pl.semaphore_signal(barrier, inc=1, device_id={"dp": sibling}, device_id_type=MESH)

    def g_copy(d, s, k):
        origin = lax.rem(t + NZ - s, NZ) if d == 0 else lax.rem(t + s, NZ)
        return _g_copy(origin, d, s, k)

    def _g_copy(origin, d, s, k):
        col = pl.multiple_of(lax.rem(origin + k, NZ) * COLS, COLS)
        ref = g_all.at[pl.ds(pl.multiple_of(origin * 32, 32), 32), pl.ds(col, COLS)]
        return pltpu.make_async_remote_copy(
            ref, ref, g_ssem.at[d, s, k], g_rsem.at[d, s, k],
            device_id={"tensor": (right, left)[d]}, device_id_type=MESH)

    def g_recv(d, s, k):
        if s >= hops(d, k):
            return
        origin = lax.rem(t + NZ - s - 1, NZ) if d == 0 else lax.rem(t + s + 1, NZ)
        _g_copy(origin, d, s, k).wait_recv()
        if s + 1 < hops(d, k):
            _g_copy(origin, d, s + 1, k).start()

    def gather(point):
        for d, s, chunks in GATHER[point]:
            for k in chunks:
                if s < 0:
                    g_copy(d, 0, k).start()
                else:
                    g_recv(d, s, k)

    def z_exchange(i, send_of, buf, prepare=None):
        for n, k in enumerate((4, 5, 3, 6, 2, 7, 1)):
            to = lax.rem(t + k, NZ)
            if prepare is not None:
                prepare(to)
                if n in (2, 4):
                    gather("prepare%d" % n)
            pltpu.make_async_remote_copy(send_of(to), buf.at[t], z_ssem.at[i], z_rsem.at[i],
                                         device_id={"tensor": to}, device_id_type=MESH).start()

    def z_wait(i, buf):
        w = buf.at[pl.ds(0, NZ - 1)]
        pltpu.make_async_copy(w, w, z_rsem.at[i]).wait()

    def pair_copy(i, send, buf):
        return pltpu.make_async_remote_copy(send, buf, pair_ssem.at[i], pair_rsem.at[i],
                                            device_id={"dp": sibling}, device_id_type=MESH)

    def dp_exchange(i, send, buf):
        for dx, dy in FAR_FIRST:
            to = lax.rem(x + dx, 4) * 8 + lax.rem(y + dy, 4) * 2 + core
            pltpu.make_async_remote_copy(send, buf.at[chip], d_ssem.at[i], d_rsem.at[i],
                                         device_id={"dp": to}, device_id_type=MESH).start()

    def dp_wait(i, buf):
        w = buf.at[pl.ds(0, CHIPS - 1)]
        pltpu.make_async_copy(w, w, d_rsem.at[i]).wait()

    load_w.wait()
    we_ref[...] = split16(w_ref[...])
    load_g.wait()
    g_own = g_all[pl.ds(pl.multiple_of(t * 32, 32), 32), :]
    p = fold(dot(we_ref[...], g_own, NT))
    wide = jnp.concatenate([p] * 4, axis=1)
    lane = lax.broadcasted_iota(jnp.int32, (4, 128), 1)
    wide = jnp.where(lane // 32 == lax.rem(t, 4), wide, 0.0)
    p_send[...] = wide
    p_buf[t] = wide

    pl.semaphore_wait(barrier, CHIPS + NZ - 1)

    z_exchange(0, lambda to: p_send, p_buf)
    gather("start")

    load_e.wait()
    left_e = jnp.zeros((16, 384), F32)
    for c in range(NZ):
        cols = pl.ds(c * COLS, COLS)
        left_e = left_e + dot(we_ref[:, cols], e_ref[:, cols], NT)
        if c == 3:
            gather("middle")
    load_a.wait()
    at_ref[...] = jnp.transpose(a_ref[...])

    gather("left")

    z_wait(0, p_buf)
    p_all = jnp.concatenate([p_buf[0] + p_buf[1] + p_buf[2] + p_buf[3], p_buf[4] + p_buf[5] + p_buf[6] + p_buf[7]], axis=1)
    left_part = fold(left_e) + fold(dot(split16(p_all), a_ref[...], NN))
    l_pair[0] = left_part
    pair_copy(0, l_pair.at[0], l_pair.at[1]).start()
    gather("pair0")
    pair_copy(0, l_pair.at[0], l_pair.at[1]).wait_recv()
    left_part = left_part + l_pair[1]
    l_send[...] = left_part
    l_buf[chip] = left_part
    dp_exchange(0, l_send, l_buf)
    gather("sent0")

    dp_wait(0, l_buf)
    lm = l_buf[0]
    for i in range(1, CHIPS):
        lm = lm + l_buf[i]
    lm = lm * (1.0 / DP)
    peak = jnp.maximum(jnp.max(jnp.abs(lm), axis=1, keepdims=True), 1e-30)
    lm = lm * (1.0 / peak)
    l16 = split16(lm)
    gram = fold(dot(l16, l16, NT))
    gram = gram[:, 0:4] + gram[:, 4:8] + gram[:, 8:12]
    info = jnp.concatenate([gram, jnp.broadcast_to(peak, (4, 124))], axis=1)
    q = fold(dot(l16, a_ref[...], NT))
    def prepare(to):
        z_send[to, :, 640:896] = q
        z_send[to, :, 896:1024] = info
        z_send[to, :, 0:640] = fold(dot(l16, e_ref[:, pl.ds(pl.multiple_of(to * COLS, COLS), COLS)], NN))

    z_exchange(1, lambda to: z_send.at[to], z_buf, prepare)
    prepare(t)
    z_buf[t] = z_send[t]

    gather("sums")

    z_wait(1, z_buf)
    peaks = [z_buf[i, :, 1000:1001] for i in range(NZ)]
    top = peaks[0]
    for i in range(1, NZ):
        top = jnp.maximum(top, peaks[i])
    inv = 1.0 / top
    scales = [x * inv for x in peaks]
    total = z_buf[0, :, 0:896] * scales[0]
    for i in range(1, NZ):
        total = total + z_buf[i, :, 0:896] * scales[i]
    gather("mine")
    mine = pl.ds(pl.multiple_of(t * COLS, COLS), COLS)
    right_part = total[:, 0:640] + fold(dot(split16(total[:, 640:896]), g_all[:, mine], NN))
    r_pair[0] = right_part
    pair_copy(1, r_pair.at[0], r_pair.at[1]).start()
    gather("pair1")
    pair_copy(1, r_pair.at[0], r_pair.at[1]).wait_recv()
    right_part = right_part + r_pair[1]
    r_send[...] = right_part
    r_buf[chip] = right_part
    dp_exchange(1, r_send, r_buf)

    diagonal = lax.broadcasted_iota(jnp.int32, (4, 4), 0) == lax.broadcasted_iota(jnp.int32, (4, 4), 1)
    gram = jnp.zeros((4, 4), F32)
    for i in range(NZ):
        across = jnp.sum(jnp.where(diagonal, scales[i], 0.0), axis=0, keepdims=True)
        gram = gram + z_buf[i, :, 896:900] * scales[i] * across
    lower = [[None] * 4 for _ in range(4)]
    inverse = [None] * 4
    for i in range(4):
        for j in range(i + 1):
            v = gram[i:i + 1, j:j + 1]
            for k in range(j):
                v = v - lower[i][k] * lower[j][k]
            lower[i][j] = jnp.sqrt(v) if i == j else v * inverse[j]
        inverse[i] = 1.0 / lower[i][i]

    rows = lm * (peak * inv)
    lo = []
    for j in range(4):
        v = rows[j:j + 1]
        for i in range(j):
            v = v - lo[i] * lower[j][i]
        lo.append(v * inverse[j])
    both = [None] * 4
    for j in (3, 2, 1, 0):
        v = lo[j]
        for i in range(j + 1, 4):
            v = v - both[i] * lower[i][j]
        both[j] = v * inverse[j]
    high, middle, low = parts3(jnp.concatenate(both, axis=0))
    zero = jnp.zeros_like(high)
    lx_ref[...] = jnp.concatenate([high, high, middle, middle, high, low, zero, zero], axis=0).astype(BF)
    flat = [lower[i][j] if i != j else inverse[i] for i in range(4) for j in range(4) if j <= i]
    for i, v in enumerate(flat):
        ch_ref[i:i + 1, :] = jnp.broadcast_to(v, (1, 128))

    gather("sent1")
    dp_wait(1, r_buf)
    nr = r_buf[0]
    for i in range(1, CHIPS):
        nr = nr + r_buf[i]
    nr = nr * (1.0 / DP)
    n_send[...] = nr
    n_buf[t] = nr
    z_exchange(2, lambda to: n_send, n_buf)

    gather("rest")

    def matrix(chunk):
        cols = pl.ds(pl.multiple_of(lax.rem(chunk, NZ) * COLS, COLS), COLS)
        m_ref[:, cols] = dot(at_ref[...], g_all[:, cols], NN) + e_ref[:, cols].astype(F32)

    matrix(t)
    for d, k in ((0, 3), (1, 5), (0, 2), (1, 6), (0, 1), (1, 7), (1, 0)):
        g_recv(d, 3, k)
        matrix(t + 4 + k)

    for d in range(2):
        for k in range(NZ):
            for s in range(hops(d, k)):
                g_copy(d, s, k).wait_send()
    pair_copy(0, l_pair.at[0], l_pair.at[1]).wait_send()
    pair_copy(1, r_pair.at[0], r_pair.at[1]).wait_send()
    for i, buf in enumerate((l_buf, r_buf)):
        w = buf.at[pl.ds(0, CHIPS - 1)]
        pltpu.make_async_copy(w, w, d_ssem.at[i]).wait()
    for i, buf in enumerate((p_buf, z_buf, n_buf)):
        w = buf.at[pl.ds(0, NZ - 1)]
        pltpu.make_async_copy(w, w, z_ssem.at[i]).wait()
    z_wait(2, n_buf)
    for c in range(NZ):
        nx_ref[:, c * COLS:(c + 1) * COLS] = n_buf[c]


def finish_kernel(m_ref, n_ref, lx_ref, ch_ref, rebuilt_hbm, error_hbm, nout_ref, out_a, out_b, sem):
    lxt = lx_ref[...]
    copies = []
    for c in range(NZ):
        cols = slice(c * COLS, (c + 1) * COLS)
        high, middle, low = parts3(n_ref[:, cols])
        zero = jnp.zeros_like(high)
        nx = jnp.concatenate([high, middle, high, middle, low, high, zero, zero], axis=0).astype(BF)
        rebuilt = dot(lxt, nx, TN)
        out_a[:, cols] = rebuilt.astype(BF)
        out_b[:, cols] = (m_ref[:, cols] - rebuilt).astype(BF)
        for i, (src, dst) in enumerate(((out_a, rebuilt_hbm), (out_b, error_hbm))):
            cp = pltpu.make_async_copy(src.at[:, cols], dst.at[:, cols], sem.at[i, c])
            cp.start()
            copies.append(cp)
    ch = [ch_ref[i:i + 1, 0:1] for i in range(10)]
    out = []
    for j in range(4):
        v = n_ref[j:j + 1, :]
        for i in range(j):
            v = v - out[i] * ch[j * (j + 1) // 2 + i]
        out.append(v * ch[j * (j + 1) // 2 + j])
        nout_ref[j:j + 1, :] = out[j]
    for cp in copies:
        cp.wait()


def per_device(activations, out_grads, error_buffer, warm_factor):
    any_spec = pl.BlockSpec(memory_space=pl.ANY)
    hbm_spec = pl.BlockSpec(memory_space=pltpu.HBM)
    vmem = pl.BlockSpec(memory_space=pltpu.VMEM)
    V = pltpu.VMEM
    D = pltpu.SemaphoreType.DMA
    m, n, lx, ch = pl.pallas_call(
        chain_kernel,
        out_shape=OUT_SHAPES(),
        in_specs=[hbm_spec] * 4,
        out_specs=[vmem] * 4,
        scratch_shapes=[
            V((256, 384), BF), V((384, 256), BF), V((384, 5120), BF), V((4, 5120), F32), V((256, 5120), BF), V((16, 5120), BF),
            V((4, 128), F32), V((NZ, 4, 128), F32), V((2, 4, 384), F32), V((4, 384), F32), V((CHIPS, 4, 384), F32),
            V((NZ, 4, 1024), F32), V((NZ, 4, 1024), F32), V((2, 4, 640), F32), V((4, 640), F32), V((CHIPS, 4, 640), F32),
            V((4, 640), F32), V((NZ, 4, 640), F32),
            D((4,)), D((2, 4, NZ)), D((2, 4, NZ)), D((3,)), D((3,)), D((2,)), D((2,)), D((2,)), D((2,)),
        ],
        compiler_params=pltpu.CompilerParams(collective_id=0, has_side_effects=True, vmem_limit_bytes=32 << 20),
    )(*(pltpu.with_memory_space_constraint(x, pltpu.HBM)
        for x in (activations[0], out_grads[0], error_buffer[0], warm_factor.T)))
    rebuilt, error, factor = pl.pallas_call(
        finish_kernel,
        out_shape=[jax.ShapeDtypeStruct((384, 5120), BF), jax.ShapeDtypeStruct((384, 5120), BF),
                   jax.ShapeDtypeStruct((4, 5120), F32)],
        in_specs=[vmem] * 4,
        out_specs=[any_spec, any_spec, vmem],
        scratch_shapes=[V((384, 5120), BF), V((384, 5120), BF), D((2, NZ))],
        compiler_params=pltpu.CompilerParams(vmem_limit_bytes=32 << 20),
    )(m, n, lx, ch)
    return rebuilt, error[None], factor.T


def OUT_SHAPES():
    return [jax.ShapeDtypeStruct((384, 5120), F32), jax.ShapeDtypeStruct((4, 5120), F32),
            jax.ShapeDtypeStruct((32, 384), BF), jax.ShapeDtypeStruct((16, 128), F32)]


def solution(mesh):
    return jax.shard_map(
        per_device,
        mesh=mesh,
        in_specs=(P("dp", None, "tensor"), P("dp", "tensor", None), P("dp", "tensor", None), P()),
        out_specs=(P("tensor", None), P("dp", "tensor", None), P()),
        check_vma=False,
    )
```

```python
import functools

import jax
import jax.numpy as jnp
from jax import lax
from jax.experimental import pallas as pl
from jax.experimental.pallas import tpu as pltpu
from jax.sharding import PartitionSpec as P

MESH = pl.DeviceIdType.MESH
F32 = jnp.float32
BF = jnp.bfloat16
DP = 32
NZ = 8
COLS = 640
NN = (((1,), (0,)), ((), ()))
NT = (((1,), (1,)), ((), ()))
TN = (((0,), (0,)), ((), ()))

RIGHT_HOPS = {0: 3, 1: 4, 2: 4, 3: 4, 4: 4, 5: 3, 6: 3, 7: 3}
CHIPS = 16
FAR_FIRST = sorted(((dx, dy) for dx in range(4) for dy in range(4) if dx or dy),
                   key=lambda v: -(min(v[0], 4 - v[0]) + min(v[1], 4 - v[1])))
GATHER = {
    "start": ((0, -1, (4, 3, 2, 1, )), (1, -1, (5, 6, 7, )), (0, -1, (0, 7, )), (1, -1, (0, 4, 3, ))),
    "middle": (),
    "left": ((0, 0, (4, 3, )), (1, 0, (5, ))),
    "pair0": ((0, 0, (2, )), (1, 0, (6, )), (0, -1, (6, 5, )), (1, -1, (2, 1, ))),
    "sent0": ((0, 1, (4, 3, )), (1, 1, (5, )), (0, 0, (1, 0, 7, )), (1, 0, (7, 0, 4, ))),
    "prepare2": (),
    "prepare4": (),
    "sums": ((0, 2, (4, )), (0, 0, (6, 5, )), (1, 0, (3, 2, 1, )), (0, 1, (2, 1, )), (1, 1, (6, 7, ))),
    "mine": ((0, 3, (4, )), (0, 2, (3, )), (1, 2, (5, ))),
    "pair1": ((0, 1, (0, 7, 6, )), (1, 1, (0, 4, 3, ))),
    "sent1": ((0, 1, (5, )), (1, 1, (2, 1, )), (0, 2, (2, 1, )), (1, 2, (6, 7, 0, ))),
    "rest": ((0, 2, (0, 7, 6, 5, )), (1, 2, (4, 3, 2, 1, ))),
}


def hops(direction, k):
    return RIGHT_HOPS[k] if direction == 0 else 7 - RIGHT_HOPS[k]


def dot(a, b, dims):
    return lax.dot_general(a, b, dims, preferred_element_type=F32)


def split16(x):
    r = jnp.concatenate([x, x, x, x], axis=0)
    high = r.astype(BF).astype(F32)
    rest = r - high
    middle = rest.astype(BF).astype(F32)
    low = rest - middle
    row = lax.broadcasted_iota(jnp.int32, r.shape, 0)
    out = jnp.where(row < 4, high, jnp.where(row < 8, middle, jnp.where(row < 12, low, 0.0)))
    return out.astype(BF)


def fold(x):
    return x[0:4] + x[4:8] + x[8:12]


def parts3(x):
    high = x.astype(BF).astype(F32)
    rest = x - high
    middle = rest.astype(BF).astype(F32)
    return high, middle, rest - middle


def chain_kernel(a_hbm, g_hbm, e_hbm, w_hbm, m_ref, nx_ref, lx_ref, ch_ref,
                 a_ref, at_ref, e_ref, w_ref, g_all, we_ref,
                 p_send, p_buf, l_pair, l_send, l_buf, z_send, z_buf, r_pair, r_send, r_buf, n_send, n_buf,
                 load_sem, g_ssem, g_rsem, z_ssem, z_rsem, d_ssem, d_rsem, pair_ssem, pair_rsem):
    t = lax.axis_index("tensor")
    r = lax.axis_index("dp")
    right, left = lax.rem(t + 1, NZ), lax.rem(t + NZ - 1, NZ)
    x, y, core = r // 8, lax.rem(r // 2, 4), lax.rem(r, 2)
    chip = r // 2
    sibling = r + 1 - 2 * core

    barrier = pltpu.get_barrier_semaphore()
    for k in (4, 5, 3, 6, 2, 7, 1):
        pl.semaphore_signal(barrier, inc=1, device_id={"tensor": lax.rem(t + k, NZ)}, device_id_type=MESH)

    load_g = pltpu.make_async_copy(g_hbm, g_all.at[pl.ds(pl.multiple_of(t * 32, 32), 32)], load_sem.at[0])
    load_w = pltpu.make_async_copy(w_hbm, w_ref, load_sem.at[1])
    load_a = pltpu.make_async_copy(a_hbm, a_ref, load_sem.at[2])
    load_e = pltpu.make_async_copy(e_hbm, e_ref, load_sem.at[3])
    for c in (load_g, load_w, load_e, load_a):
        c.start()
    for dx, dy in FAR_FIRST:
        to = lax.rem(x + dx, 4) * 8 + lax.rem(y + dy, 4) * 2 + core
        pl.semaphore_signal(barrier, inc=1, device_id={"dp": to}, device_id_type=MESH)
    pl.semaphore_signal(barrier, inc=1, device_id={"dp": sibling}, device_id_type=MESH)

    def g_copy(d, s, k):
        origin = lax.rem(t + NZ - s, NZ) if d == 0 else lax.rem(t + s, NZ)
        return _g_copy(origin, d, s, k)

    def _g_copy(origin, d, s, k):
        col = pl.multiple_of(lax.rem(origin + k, NZ) * COLS, COLS)
        ref = g_all.at[pl.ds(pl.multiple_of(origin * 32, 32), 32), pl.ds(col, COLS)]
        return pltpu.make_async_remote_copy(
            ref, ref, g_ssem.at[d, s, k], g_rsem.at[d, s, k],
            device_id={"tensor": (right, left)[d]}, device_id_type=MESH)

    def g_recv(d, s, k):
        if s >= hops(d, k):
            return
        origin = lax.rem(t + NZ - s - 1, NZ) if d == 0 else lax.rem(t + s + 1, NZ)
        _g_copy(origin, d, s, k).wait_recv()
        if s + 1 < hops(d, k):
            _g_copy(origin, d, s + 1, k).start()

    def gather(point):
        for d, s, chunks in GATHER[point]:
            for k in chunks:
                if s < 0:
                    g_copy(d, 0, k).start()
                else:
                    g_recv(d, s, k)

    def z_exchange(i, send_of, buf, prepare=None):
        for n, k in enumerate((4, 5, 3, 6, 2, 7, 1)):
            to = lax.rem(t + k, NZ)
            if prepare is not None:
                prepare(to)
                if n in (2, 4):
                    gather("prepare%d" % n)
            pltpu.make_async_remote_copy(send_of(to), buf.at[t], z_ssem.at[i], z_rsem.at[i],
                                         device_id={"tensor": to}, device_id_type=MESH).start()

    def z_wait(i, buf):
        w = buf.at[pl.ds(0, NZ - 1)]
        pltpu.make_async_copy(w, w, z_rsem.at[i]).wait()

    def pair_copy(i, send, buf):
        return pltpu.make_async_remote_copy(send, buf, pair_ssem.at[i], pair_rsem.at[i],
                                            device_id={"dp": sibling}, device_id_type=MESH)

    def dp_exchange(i, send, buf):
        for dx, dy in FAR_FIRST:
            to = lax.rem(x + dx, 4) * 8 + lax.rem(y + dy, 4) * 2 + core
            pltpu.make_async_remote_copy(send, buf.at[chip], d_ssem.at[i], d_rsem.at[i],
                                         device_id={"dp": to}, device_id_type=MESH).start()

    def dp_wait(i, buf):
        w = buf.at[pl.ds(0, CHIPS - 1)]
        pltpu.make_async_copy(w, w, d_rsem.at[i]).wait()

    load_w.wait()
    we_ref[...] = split16(w_ref[...])
    load_g.wait()
    g_own = g_all[pl.ds(pl.multiple_of(t * 32, 32), 32), :]
    p = fold(dot(we_ref[...], g_own, NT))
    wide = jnp.concatenate([p] * 4, axis=1)
    lane = lax.broadcasted_iota(jnp.int32, (4, 128), 1)
    wide = jnp.where(lane // 32 == lax.rem(t, 4), wide, 0.0)
    p_send[...] = wide
    p_buf[t] = wide

    pl.semaphore_wait(barrier, CHIPS + NZ - 1)

    z_exchange(0, lambda to: p_send, p_buf)
    gather("start")

    load_e.wait()
    left_e = jnp.zeros((16, 384), F32)
    for c in range(NZ):
        cols = pl.ds(c * COLS, COLS)
        left_e = left_e + dot(we_ref[:, cols], e_ref[:, cols], NT)
        if c == 3:
            gather("middle")
    load_a.wait()
    at_ref[...] = jnp.transpose(a_ref[...])

    gather("left")

    z_wait(0, p_buf)
    p_all = jnp.concatenate([p_buf[0] + p_buf[1] + p_buf[2] + p_buf[3], p_buf[4] + p_buf[5] + p_buf[6] + p_buf[7]], axis=1)
    left_part = fold(left_e) + fold(dot(split16(p_all), a_ref[...], NN))
    l_pair[0] = left_part
    pair_copy(0, l_pair.at[0], l_pair.at[1]).start()
    gather("pair0")
    pair_copy(0, l_pair.at[0], l_pair.at[1]).wait_recv()
    left_part = left_part + l_pair[1]
    l_send[...] = left_part
    l_buf[chip] = left_part
    dp_exchange(0, l_send, l_buf)
    gather("sent0")

    dp_wait(0, l_buf)
    lm = l_buf[0]
    for i in range(1, CHIPS):
        lm = lm + l_buf[i]
    lm = lm * (1.0 / DP)
    peak = jnp.maximum(jnp.max(jnp.abs(lm), axis=1, keepdims=True), 1e-30)
    lm = lm * (1.0 / peak)
    l16 = split16(lm)
    gram = fold(dot(l16, l16, NT))
    gram = gram[:, 0:4] + gram[:, 4:8] + gram[:, 8:12]
    info = jnp.concatenate([gram, jnp.broadcast_to(peak, (4, 124))], axis=1)
    q = fold(dot(l16, a_ref[...], NT))
    def prepare(to):
        z_send[to, :, 640:896] = q
        z_send[to, :, 896:1024] = info
        z_send[to, :, 0:640] = fold(dot(l16, e_ref[:, pl.ds(pl.multiple_of(to * COLS, COLS), COLS)], NN))

    z_exchange(1, lambda to: z_send.at[to], z_buf, prepare)
    prepare(t)
    z_buf[t] = z_send[t]

    gather("sums")

    z_wait(1, z_buf)
    peaks = [z_buf[i, :, 1000:1001] for i in range(NZ)]
    top = peaks[0]
    for i in range(1, NZ):
        top = jnp.maximum(top, peaks[i])
    inv = 1.0 / top
    scales = [x * inv for x in peaks]
    total = z_buf[0, :, 0:896] * scales[0]
    for i in range(1, NZ):
        total = total + z_buf[i, :, 0:896] * scales[i]
    gather("mine")
    mine = pl.ds(pl.multiple_of(t * COLS, COLS), COLS)
    right_part = total[:, 0:640] + fold(dot(split16(total[:, 640:896]), g_all[:, mine], NN))
    r_pair[0] = right_part
    pair_copy(1, r_pair.at[0], r_pair.at[1]).start()
    gather("pair1")
    pair_copy(1, r_pair.at[0], r_pair.at[1]).wait_recv()
    right_part = right_part + r_pair[1]
    r_send[...] = right_part
    r_buf[chip] = right_part
    dp_exchange(1, r_send, r_buf)

    diagonal = lax.broadcasted_iota(jnp.int32, (4, 4), 0) == lax.broadcasted_iota(jnp.int32, (4, 4), 1)
    gram = jnp.zeros((4, 4), F32)
    for i in range(NZ):
        across = jnp.sum(jnp.where(diagonal, scales[i], 0.0), axis=0, keepdims=True)
        gram = gram + z_buf[i, :, 896:900] * scales[i] * across
    lower = [[None] * 4 for _ in range(4)]
    inverse = [None] * 4
    for i in range(4):
        for j in range(i + 1):
            v = gram[i:i + 1, j:j + 1]
            for k in range(j):
                v = v - lower[i][k] * lower[j][k]
            lower[i][j] = jnp.sqrt(v) if i == j else v * inverse[j]
        inverse[i] = 1.0 / lower[i][i]

    rows = lm * (peak * inv)
    lo = []
    for j in range(4):
        v = rows[j:j + 1]
        for i in range(j):
            v = v - lo[i] * lower[j][i]
        lo.append(v * inverse[j])
    both = [None] * 4
    for j in (3, 2, 1, 0):
        v = lo[j]
        for i in range(j + 1, 4):
            v = v - both[i] * lower[i][j]
        both[j] = v * inverse[j]
    high, middle, low = parts3(jnp.concatenate(both, axis=0))
    zero = jnp.zeros_like(high)
    lx_ref[...] = jnp.concatenate([high, high, middle, middle, high, low, zero, zero], axis=0).astype(BF)
    flat = [lower[i][j] if i != j else inverse[i] for i in range(4) for j in range(4) if j <= i]
    for i, v in enumerate(flat):
        ch_ref[i:i + 1, :] = jnp.broadcast_to(v, (1, 128))

    gather("sent1")
    dp_wait(1, r_buf)
    nr = r_buf[0]
    for i in range(1, CHIPS):
        nr = nr + r_buf[i]
    nr = nr * (1.0 / DP)
    n_send[...] = nr
    n_buf[t] = nr
    z_exchange(2, lambda to: n_send, n_buf)

    gather("rest")

    def matrix(chunk):
        cols = pl.ds(pl.multiple_of(lax.rem(chunk, NZ) * COLS, COLS), COLS)
        m_ref[:, cols] = dot(at_ref[...], g_all[:, cols], NN) + e_ref[:, cols].astype(F32)

    matrix(t)
    for d, k in ((0, 3), (1, 5), (0, 2), (1, 6), (0, 1), (1, 7), (1, 0)):
        g_recv(d, 3, k)
        matrix(t + 4 + k)

    for d in range(2):
        for k in range(NZ):
            for s in range(hops(d, k)):
                g_copy(d, s, k).wait_send()
    pair_copy(0, l_pair.at[0], l_pair.at[1]).wait_send()
    pair_copy(1, r_pair.at[0], r_pair.at[1]).wait_send()
    for i, buf in enumerate((l_buf, r_buf)):
        w = buf.at[pl.ds(0, CHIPS - 1)]
        pltpu.make_async_copy(w, w, d_ssem.at[i]).wait()
    for i, buf in enumerate((p_buf, z_buf, n_buf)):
        w = buf.at[pl.ds(0, NZ - 1)]
        pltpu.make_async_copy(w, w, z_ssem.at[i]).wait()
    z_wait(2, n_buf)
    for c in range(NZ):
        nx_ref[:, c * COLS:(c + 1) * COLS] = n_buf[c]


def finish_kernel(m_ref, n_ref, lx_ref, ch_ref, rebuilt_hbm, error_hbm, nout_ref, out_a, out_b, sem):
    lxt = lx_ref[...]
    copies = []
    for c in range(NZ):
        cols = slice(c * COLS, (c + 1) * COLS)
        high, middle, low = parts3(n_ref[:, cols])
        zero = jnp.zeros_like(high)
        nx = jnp.concatenate([high, middle, high, middle, low, high, zero, zero], axis=0).astype(BF)
        rebuilt = dot(lxt, nx, TN)
        out_a[:, cols] = rebuilt.astype(BF)
        out_b[:, cols] = (m_ref[:, cols] - rebuilt).astype(BF)
        for i, (src, dst) in enumerate(((out_a, rebuilt_hbm), (out_b, error_hbm))):
            cp = pltpu.make_async_copy(src.at[:, cols], dst.at[:, cols], sem.at[i, c])
            cp.start()
            copies.append(cp)
    ch = [ch_ref[i:i + 1, 0:1] for i in range(10)]
    out = []
    for j in range(4):
        v = n_ref[j:j + 1, :]
        for i in range(j):
            v = v - out[i] * ch[j * (j + 1) // 2 + i]
        out.append(v * ch[j * (j + 1) // 2 + j])
        nout_ref[j:j + 1, :] = out[j]
    for cp in copies:
        cp.wait()


def per_device(activations, out_grads, error_buffer, warm_factor):
    any_spec = pl.BlockSpec(memory_space=pl.ANY)
    hbm_spec = pl.BlockSpec(memory_space=pltpu.HBM)
    vmem = pl.BlockSpec(memory_space=pltpu.VMEM)
    V = pltpu.VMEM
    D = pltpu.SemaphoreType.DMA
    m, n, lx, ch = pl.pallas_call(
        chain_kernel,
        out_shape=OUT_SHAPES(),
        in_specs=[hbm_spec] * 4,
        out_specs=[vmem] * 4,
        scratch_shapes=[
            V((256, 384), BF), V((384, 256), BF), V((384, 5120), BF), V((4, 5120), F32), V((256, 5120), BF), V((16, 5120), BF),
            V((4, 128), F32), V((NZ, 4, 128), F32), V((2, 4, 384), F32), V((4, 384), F32), V((CHIPS, 4, 384), F32),
            V((NZ, 4, 1024), F32), V((NZ, 4, 1024), F32), V((2, 4, 640), F32), V((4, 640), F32), V((CHIPS, 4, 640), F32),
            V((4, 640), F32), V((NZ, 4, 640), F32),
            D((4,)), D((2, 4, NZ)), D((2, 4, NZ)), D((3,)), D((3,)), D((2,)), D((2,)), D((2,)), D((2,)),
        ],
        compiler_params=pltpu.CompilerParams(collective_id=0, has_side_effects=True, vmem_limit_bytes=32 << 20),
    )(*(pltpu.with_memory_space_constraint(x, pltpu.HBM)
        for x in (activations[0], out_grads[0], error_buffer[0], warm_factor.T)))
    rebuilt, error, factor = pl.pallas_call(
        finish_kernel,
        out_shape=[jax.ShapeDtypeStruct((384, 5120), BF), jax.ShapeDtypeStruct((384, 5120), BF),
                   jax.ShapeDtypeStruct((4, 5120), F32)],
        in_specs=[vmem] * 4,
        out_specs=[any_spec, any_spec, vmem],
        scratch_shapes=[V((384, 5120), BF), V((384, 5120), BF), D((2, NZ))],
        compiler_params=pltpu.CompilerParams(vmem_limit_bytes=32 << 20),
    )(m, n, lx, ch)
    return rebuilt, error[None], factor.T


def OUT_SHAPES():
    return [jax.ShapeDtypeStruct((384, 5120), F32), jax.ShapeDtypeStruct((4, 5120), F32),
            jax.ShapeDtypeStruct((32, 384), BF), jax.ShapeDtypeStruct((16, 128), F32)]


def solution(mesh):
    return jax.shard_map(
        per_device,
        mesh=mesh,
        in_specs=(P("dp", None, "tensor"), P("dp", "tensor", None), P("dp", "tensor", None), P()),
        out_specs=(P("tensor", None), P("dp", "tensor", None), P()),
        check_vma=False,
    )
```
